32 devices in a mesh: blk: 4 (over y, x), grp: 8 (over z, core).
Axes of the slice: x: 2, y: 2, z: 4, core: 2. Of those that a mesh axis runs over, the one named last changes fastest.
Arguments:
- amplitudes: bfloat16 [256, 6144], P(('blk', 'grp')), may hold values from -6 to 6
- integrals: bfloat16 [6144, 512], P('grp', 'blk'), may hold values from -0.109375 to 0.109375
- tile_mask: int32 [32, 48], P(('blk', 'grp')), may hold values from 0 to 1, as said below
- tile_size: int32 [48], replicated, may hold values from 64 to 128, as said below
Outputs:
- ladder: bfloat16 [256, 512], P(('blk', 'grp'))
The draws below stay inside these ranges and needn't reach their ends.
Inputs may be any that keep to these rules, and one draw needn't show every extreme that they name: `tile_mask`: mask entries are 0 or 1; domains differ in how many of their tiles are live. `tile_size`: one tile is full and one is half full.
All inputs are finite; a program needn't handle non-finite values.
Results may differ from the reference program's by a relative error of at most 0.001.
Values may be sent and summed in bfloat16 or wider, within the bound.
No kernel may reach another device: no remote copies, remote signals or barrier semaphores. Data moves between devices by JAX's collectives and lax.ppermute only.
A program may use at most 64 MiB of HBM per device.

```python
import math
import jax
import jax.numpy as jnp
from jax import lax

TILE = 128
ROWS_DEV = 8
DOMAINS = 32
ROWS = 256
NTILES = 48
NCD = 6144
NAB = 512


def draw_tile_mask(key, part):
    level_key = jax.random.fold_in(key, 11)
    entry_key = jax.random.fold_in(key, 23)
    level = jax.random.randint(level_key, (DOMAINS, 1), 3, 9)
    entries = jax.random.randint(entry_key, (DOMAINS, NTILES), 0, 8)
    mask_values = (entries < level).astype(jnp.int32)
    mask_values = mask_values.at[0, 0].set(1)
    mask_values = mask_values.at[0, 1].set(0)
    return mask_values


def draw_tile_size(key, part):
    size_key = jax.random.fold_in(key, 37)
    sizes = jax.random.randint(size_key, (NTILES,), TILE // 2, TILE + 1)
    sizes = sizes.at[0].set(TILE)
    sizes = sizes.at[1].set(TILE // 2)
    return sizes.astype(jnp.int32)


def levels(key, dims, pieces, smallest, high):
    gain = 1.0
    for dim, parts in pieces:
        draws = jax.random.uniform(jax.random.fold_in(jax.random.fold_in(key, 6), dim), (parts,), jnp.float32, smallest / len(pieces), high / len(pieces))
        gain = gain * jnp.repeat(jnp.exp(draws), dims[dim] // parts).reshape((-1,) + (1,) * (len(dims) - 1 - dim))
    return gain


def centred(rng, extent, spread, most, pieces=(), kind=jnp.bfloat16):
    values = spread * jax.random.normal(rng, extent, jnp.float32)
    if pieces:
        values = values * levels(rng, extent, pieces, -0.22, 0.18)
    return jnp.clip(values, -most, most).astype(kind)


def setup_inputs(seed: int = 0) -> dict:
    splits = jax.random.split(jax.random.key(seed), 5)
    return {
        "amplitudes": centred(splits[0], (ROWS, NCD), 1.0, 6.0, ((0, 32),)),
        "integrals": centred(splits[1], (NCD, NAB), (NCD // 2) ** -0.5, 0.109375, ((0, 8), (1, 4))),
        "tile_mask": draw_tile_mask(jax.random.fold_in(splits[4], 71), 0),
        "tile_size": draw_tile_size(jax.random.fold_in(splits[4], 71), 0),
    }


def reference(amplitudes, integrals, tile_mask, tile_size):
    width = amplitudes.shape[1]
    column = jnp.arange(width, dtype=jnp.int32)
    tile_of = column // TILE
    column_live = (column % TILE) < tile_size[tile_of]
    group = math.gcd(DOMAINS, 64)
    amp_blocks = amplitudes.reshape(DOMAINS // group, group * ROWS_DEV, width)
    mask_blocks = tile_mask.reshape(DOMAINS // group, group, NTILES)

    def one_block(pair):
        amp_rows, mask_rows = pair
        domain_live = mask_rows[:, tile_of] == 1
        domain_live = jnp.repeat(domain_live, ROWS_DEV, axis=0)
        live = domain_live & column_live[None, :]
        masked = jnp.where(live, amp_rows, jnp.zeros_like(amp_rows))
        return jnp.dot(masked, integrals, preferred_element_type=jnp.float32).astype(jnp.bfloat16)

    result = lax.map(one_block, (amp_blocks, mask_blocks))
    return result.reshape(ROWS, NAB)
```

```python
import functools

import jax
import jax.numpy as jnp
from jax import lax
from jax.experimental import pallas as pl
from jax.experimental.pallas import tpu as pltpu
from jax.sharding import PartitionSpec as P

CORES = 2
VMEM = pl.BlockSpec(memory_space=pltpu.VMEM)
SMEM = pl.BlockSpec(memory_space=pltpu.SMEM)


def mask_kernel(order, mask_ref, size_ref, amplitude_ref, *out_refs):
    grp = lax.axis_index("grp")
    chip, core = grp // CORES, lax.rem(grp, CORES)
    rows, width = amplitude_ref.shape
    tile = width // size_ref.shape[0]
    tiles = out_refs[0].shape[1] // tile // CORES
    lane = lax.broadcasted_iota(jnp.int32, (rows, tile), 1)
    for out_ref, step in zip(out_refs, order):
        for half in range(CORES):
            first = ((chip ^ step) * CORES + (core ^ half)) * tiles
            for t in range(tiles):
                k = first + t
                live = jnp.where(mask_ref[0, k] == 1, size_ref[k], 0)
                value = amplitude_ref[:, pl.ds(pl.multiple_of(k * tile, tile), tile)]
                place = (half * tiles + t) * tile
                out_ref[:, place : place + tile] = jnp.where(lane < live, value, jnp.zeros_like(value))


def live_blocks(amplitudes, tile_mask, tile_size, order, members):
    rows, width = amplitudes.shape
    shape = jax.ShapeDtypeStruct((rows, CORES * width // members), amplitudes.dtype)
    return pl.pallas_call(
        functools.partial(mask_kernel, order),
        out_shape=[shape] * len(order),
        in_specs=[SMEM, SMEM, VMEM],
        out_specs=[VMEM] * len(order),
        name="live_blocks",
    )(tile_mask, tile_size, amplitudes)


def body(blk_size, grp_size, amplitudes, integrals, tile_mask, tile_size):
    rows, depth, cols = amplitudes.shape[0], *integrals.shape
    chips = grp_size // CORES
    order = tuple(range(chips - 1, 0, -1))
    blk = lax.axis_index("blk")

    def between(array, axis, size, step):
        return lax.ppermute(array, axis, [(k, k ^ step) for k in range(size)])

    own = jnp.concatenate(
        [integrals] + [between(integrals, "blk", blk_size, step) for step in range(1, blk_size)], axis=1
    )
    blocks = live_blocks(amplitudes, tile_mask, tile_size, (0,) + order, grp_size)
    received = [between(b, "grp", grp_size, CORES * step) for b, step in zip(blocks[1:], order)]
    received[-1], own = lax.optimization_barrier((received[-1], own))
    other = between(own, "grp", grp_size, 1)
    live = jnp.concatenate([blocks[0]] + received, axis=0)
    partial = jnp.dot(live[:, :depth], own, preferred_element_type=jnp.float32)
    partial += jnp.dot(live[:, depth:], other, preferred_element_type=jnp.float32)
    ladder = partial[:rows]
    for place, step in enumerate(order, 1):
        ladder += between(partial[place * rows : (place + 1) * rows], "grp", grp_size, CORES * step)
    ladder = ladder.astype(jnp.bfloat16)
    pieces = [ladder[:, k * cols : (k + 1) * cols] for k in range(blk_size)]
    return jnp.concatenate([lax.select_n(blk ^ k, *pieces) for k in range(blk_size)], axis=1)


def solution(mesh):
    return jax.shard_map(
        functools.partial(body, mesh.shape["blk"], mesh.shape["grp"]),
        mesh=mesh,
        in_specs=(P(("blk", "grp"), None), P("grp", "blk"), P(("blk", "grp"), None), P()),
        out_specs=P(("blk", "grp"), None),
        check_vma=False,
    )
```

```python
import functools
import math

import jax
import jax.numpy as jnp
from jax import lax
from jax.experimental import pallas as pl
from jax.experimental.pallas import tpu as pltpu
from jax.sharding import PartitionSpec as P

CORES = 2
VMEM = pl.BlockSpec(memory_space=pltpu.VMEM)
SMEM = pl.BlockSpec(memory_space=pltpu.SMEM)


def local_call(kernel, name, out_shape, in_specs, operands, cost=None):
    arrays = [*operands, *jax.tree.leaves(out_shape)]
    held = sum(math.prod(a.shape) * a.dtype.itemsize for a in arrays)
    return pl.pallas_call(
        kernel,
        out_shape=out_shape,
        in_specs=in_specs,
        out_specs=jax.tree.map(lambda _: VMEM, out_shape),
        name=name,
        cost_estimate=cost,
        compiler_params=pltpu.CompilerParams(vmem_limit_bytes=held + (2 << 20)),
    )(*operands)


def lane_kernel(lane_ref):
    lane_ref[...] = lax.broadcasted_iota(jnp.int32, lane_ref.shape, 1)


def mask_kernel(order, lane_ref, mask_ref, size_ref, amplitude_ref, *out_refs):
    grp = lax.axis_index("grp")
    chip, core = grp // CORES, lax.rem(grp, CORES)
    lane = lane_ref[...]
    tile = lane.shape[1]
    tiles = out_refs[0].shape[1] // tile // CORES
    for out_ref, step in zip(out_refs, order):
        for half in range(CORES):
            first = ((chip ^ step) * CORES + (core ^ half)) * tiles
            for t in range(tiles):
                k = first + t
                live = jnp.where(mask_ref[0, k] == 1, size_ref[k], 0)
                value = amplitude_ref[:, pl.ds(pl.multiple_of(k * tile, tile), tile)]
                place = (half * tiles + t) * tile
                out_ref[:, place : place + tile] = jnp.where(lane < live, value, jnp.zeros_like(value))


def dot_kernel(members, blocks, *refs):
    live_refs, own_refs, other_refs = refs[:members], refs[members : members + blocks], refs[members + blocks : -1]
    out_ref = refs[-1]
    blk = lax.axis_index("blk")
    depth, cols = own_refs[0].shape
    live = jnp.concatenate([ref[...] for ref in live_refs], axis=0)
    for step, (own_ref, other_ref) in enumerate(zip(own_refs, other_refs)):
        total = jnp.dot(live[:, :depth], own_ref[...], preferred_element_type=jnp.float32)
        total += jnp.dot(live[:, depth:], other_ref[...], preferred_element_type=jnp.float32)
        out_ref[:, pl.ds(pl.multiple_of((blk ^ step) * cols, cols), cols)] = total


def after(received, places, value):
    *arrived, value = lax.optimization_barrier((*[received[k] for k in places], value))
    for k, array in zip(places, arrived):
        received[k] = array
    return value


def body(blk_size, grp_size, amplitudes, integrals, tile_mask, tile_size):
    rows, width = amplitudes.shape
    depth, cols = integrals.shape
    chips = grp_size // CORES
    chip = lax.axis_index("grp") // CORES

    def swap(array, axis, size, step):
        return lax.ppermute(array, axis, [(k, k ^ step) for k in range(size)])

    def shift(array, step):
        pairs = [(k, (k // CORES + step) % chips * CORES + k % CORES) for k in range(grp_size)]
        return lax.ppermute(array, "grp", pairs)

    own = [integrals] + [swap(integrals, "blk", blk_size, step) for step in range(1, blk_size)]

    lane = local_call(
        lane_kernel,
        "lane",
        jax.ShapeDtypeStruct((rows, width // tile_size.shape[0]), jnp.int32),
        [],
        [],
        pl.CostEstimate(flops=10**9, bytes_accessed=0, transcendentals=0),
    )
    order = (0, *range(chips - 1, 0, -1))
    block = jax.ShapeDtypeStruct((rows, CORES * depth), amplitudes.dtype)
    blocks = local_call(
        functools.partial(mask_kernel, order),
        "live_blocks",
        [block] * chips,
        [VMEM, SMEM, SMEM, VMEM],
        [lane, tile_mask, tile_size, amplitudes],
    )
    blocks = list(blocks)
    if blk_size > 1:
        blocks[-1], own[1] = lax.optimization_barrier((blocks[-1], own[1]))
    received = [blocks[0]] + [swap(b, "grp", grp_size, CORES * step) for b, step in zip(blocks[1:], order[1:])]

    other = []
    for step in range(blk_size):
        places = range(1, chips) if step > 1 else range(1, min(2, chips))
        own[step] = after(received, places, own[step])
        other.append(swap(own[step], "grp", grp_size, 1))

    partial = local_call(
        functools.partial(dot_kernel, chips, blk_size),
        "dots",
        jax.ShapeDtypeStruct((chips * rows, blk_size * cols), jnp.float32),
        [VMEM] * (chips + 2 * blk_size),
        [*received, *own, *other],
    )
    ladder = partial[:rows]
    for step in range(1, chips):
        place = chips - (chip ^ lax.rem(chip + step, chips))
        ladder += shift(lax.dynamic_slice_in_dim(partial, place * rows, rows), step)
    return ladder.astype(jnp.bfloat16)


def solution(mesh):
    return jax.shard_map(
        functools.partial(body, mesh.shape["blk"], mesh.shape["grp"]),
        mesh=mesh,
        in_specs=(P(("blk", "grp"), None), P("grp", "blk"), P(("blk", "grp"), None), P()),
        out_specs=P(("blk", "grp"), None),
        check_vma=False,
    )
```

```python
import functools
import math

import jax
import jax.numpy as jnp
from jax import lax
from jax.experimental import pallas as pl
from jax.experimental.pallas import tpu as pltpu
from jax.sharding import PartitionSpec as P

CORES = 2
VMEM = pl.BlockSpec(memory_space=pltpu.VMEM)
SMEM = pl.BlockSpec(memory_space=pltpu.SMEM)


def local_call(kernel, name, out_shape, in_specs, operands, cost=None):
    arrays = [*operands, *jax.tree.leaves(out_shape)]
    held = sum(math.prod(a.shape) * a.dtype.itemsize for a in arrays)
    return pl.pallas_call(
        kernel,
        out_shape=out_shape,
        in_specs=in_specs,
        out_specs=jax.tree.map(lambda _: VMEM, out_shape),
        name=name,
        cost_estimate=cost,
        compiler_params=pltpu.CompilerParams(vmem_limit_bytes=held + (2 << 20)),
    )(*operands)


def lane_kernel(lane_ref):
    lane_ref[...] = lax.broadcasted_iota(jnp.int32, lane_ref.shape, 1)


def mask_kernel(order, lane_ref, mask_ref, size_ref, amplitude_ref, *out_refs):
    grp = lax.axis_index("grp")
    chip, core = grp // CORES, lax.rem(grp, CORES)
    lane = lane_ref[...]
    tile = lane.shape[1]
    tiles = out_refs[0].shape[1] // tile // CORES
    for out_ref, step in zip(out_refs, order):
        for half in range(CORES):
            first = ((chip ^ step) * CORES + (core ^ half)) * tiles
            for t in range(tiles):
                k = first + t
                live = jnp.where(mask_ref[0, k] == 1, size_ref[k], 0)
                value = amplitude_ref[:, pl.ds(pl.multiple_of(k * tile, tile), tile)]
                place = (half * tiles + t) * tile
                out_ref[:, place : place + tile] = jnp.where(lane < live, value, jnp.zeros_like(value))


def dot_kernel(members, blocks, *refs):
    live_refs, own_refs, other_refs = refs[:members], refs[members : members + blocks], refs[members + blocks : -1]
    out_ref = refs[-1]
    blk = lax.axis_index("blk")
    depth, cols = own_refs[0].shape
    live = jnp.concatenate([ref[...] for ref in live_refs], axis=0)
    for step, (own_ref, other_ref) in enumerate(zip(own_refs, other_refs)):
        total = jnp.dot(live[:, :depth], own_ref[...], preferred_element_type=jnp.float32)
        total += jnp.dot(live[:, depth:], other_ref[...], preferred_element_type=jnp.float32)
        out_ref[:, pl.ds(pl.multiple_of((blk ^ step) * cols, cols), cols)] = total


def after(received, places, value):
    *arrived, value = lax.optimization_barrier((*[received[k] for k in places], value))
    for k, array in zip(places, arrived):
        received[k] = array
    return value


def body(blk_size, grp_size, amplitudes, integrals, tile_mask, tile_size):
    rows, width = amplitudes.shape
    depth, cols = integrals.shape
    chips = grp_size // CORES
    chip = lax.axis_index("grp") // CORES

    def swap(array, axis, size, step):
        return lax.ppermute(array, axis, [(k, k ^ step) for k in range(size)])

    def shift(array, step):
        pairs = [(k, (k // CORES + step) % chips * CORES + k % CORES) for k in range(grp_size)]
        return lax.ppermute(array, "grp", pairs)

    lane = local_call(
        lane_kernel,
        "lane",
        jax.ShapeDtypeStruct((rows, width // tile_size.shape[0]), jnp.int32),
        [],
        [],
        pl.CostEstimate(flops=10**9, bytes_accessed=0, transcendentals=0),
    )

    lane, later = lax.optimization_barrier((lane, integrals))
    own = [integrals] + [swap(integrals if step == 1 else later, "blk", blk_size, step) for step in range(1, blk_size)]

    order = (0, *range(chips - 1, 0, -1))
    block = jax.ShapeDtypeStruct((rows, CORES * depth), amplitudes.dtype)
    blocks = local_call(
        functools.partial(mask_kernel, order),
        "live_blocks",
        [block] * chips,
        [VMEM, SMEM, SMEM, VMEM],
        [lane, tile_mask, tile_size, amplitudes],
    )
    blocks = list(blocks)
    if blk_size > 1:
        blocks[-1], own[1] = lax.optimization_barrier((blocks[-1], own[1]))
    received = [blocks[0]] + [swap(b, "grp", grp_size, CORES * step) for b, step in zip(blocks[1:], order[1:])]

    other = []
    for step in range(blk_size):
        places = range(1, chips) if step > 1 else range(1, min(2, chips))
        own[step] = after(received, places, own[step])
        other.append(swap(own[step], "grp", grp_size, 1))

    partial = local_call(
        functools.partial(dot_kernel, chips, blk_size),
        "dots",
        jax.ShapeDtypeStruct((chips * rows, blk_size * cols), jnp.float32),
        [VMEM] * (chips + 2 * blk_size),
        [*received, *own, *other],
    )
    ladder = partial[:rows]
    for step in range(1, chips):
        place = chips - (chip ^ lax.rem(chip + step, chips))
        ladder += shift(lax.dynamic_slice_in_dim(partial, place * rows, rows), step)
    return ladder.astype(jnp.bfloat16)


def solution(mesh):
    return jax.shard_map(
        functools.partial(body, mesh.shape["blk"], mesh.shape["grp"]),
        mesh=mesh,
        in_specs=(P(("blk", "grp"), None), P("grp", "blk"), P(("blk", "grp"), None), P()),
        out_specs=P(("blk", "grp"), None),
        check_vma=False,
    )
```

```python
import functools
import math

import jax
import jax.numpy as jnp
from jax import lax
from jax.experimental import pallas as pl
from jax.experimental.pallas import tpu as pltpu
from jax.sharding import PartitionSpec as P

CORES = 2
VMEM = pl.BlockSpec(memory_space=pltpu.VMEM)
SMEM = pl.BlockSpec(memory_space=pltpu.SMEM)


def local_call(kernel, name, out_shape, in_specs, operands, cost=None):
    arrays = [*operands, *jax.tree.leaves(out_shape)]
    held = sum(math.prod(a.shape) * a.dtype.itemsize for a in arrays)
    return pl.pallas_call(
        kernel,
        out_shape=out_shape,
        in_specs=in_specs,
        out_specs=jax.tree.map(lambda _: VMEM, out_shape),
        name=name,
        cost_estimate=cost,
        compiler_params=pltpu.CompilerParams(vmem_limit_bytes=held + (2 << 20)),
    )(*operands)


def lane_kernel(lane_ref):
    lane_ref[...] = lax.broadcasted_iota(jnp.int32, lane_ref.shape, 1)


def mask_kernel(order, lane_ref, mask_ref, size_ref, amplitude_ref, *out_refs):
    grp = lax.axis_index("grp")
    chip, core = grp // CORES, lax.rem(grp, CORES)
    lane = lane_ref[...]
    tile = lane.shape[1]
    tiles = out_refs[0].shape[1] // tile // CORES
    for out_ref, step in zip(out_refs, order):
        for half in range(CORES):
            first = ((chip ^ step) * CORES + (core ^ half)) * tiles
            for t in range(tiles):
                k = first + t
                live = jnp.where(mask_ref[0, k] == 1, size_ref[k], 0)
                value = amplitude_ref[:, pl.ds(pl.multiple_of(k * tile, tile), tile)]
                place = (half * tiles + t) * tile
                out_ref[:, place : place + tile] = jnp.where(lane < live, value, jnp.zeros_like(value))


def dot_kernel(members, blocks, *refs):
    live_refs, own_refs, other_refs = refs[:members], refs[members : members + blocks], refs[members + blocks : -1]
    out_ref = refs[-1]
    blk = lax.axis_index("blk")
    depth, cols = own_refs[0].shape
    live = jnp.concatenate([ref[...] for ref in live_refs], axis=0)
    for step, (own_ref, other_ref) in enumerate(zip(own_refs, other_refs)):
        total = jnp.dot(live[:, :depth], own_ref[...], preferred_element_type=jnp.float32)
        total += jnp.dot(live[:, depth:], other_ref[...], preferred_element_type=jnp.float32)
        out_ref[:, pl.ds(pl.multiple_of((blk ^ step) * cols, cols), cols)] = total


def after(received, places, value):
    *arrived, value = lax.optimization_barrier((*[received[k] for k in places], value))
    for k, array in zip(places, arrived):
        received[k] = array
    return value


def body(blk_size, grp_size, amplitudes, integrals, tile_mask, tile_size):
    rows, width = amplitudes.shape
    depth, cols = integrals.shape
    chips = grp_size // CORES
    chip = lax.axis_index("grp") // CORES

    def swap(array, axis, size, step):
        return lax.ppermute(array, axis, [(k, k ^ step) for k in range(size)])

    ring = [k ^ (k >> 1) for k in range(chips)]
    after_chip = [[ring[(ring.index(k) + step) % chips] for k in range(chips)] for step in range(chips)]

    def shift(array, step):
        pairs = [(k, after_chip[step][k // CORES] * CORES + k % CORES) for k in range(grp_size)]
        return lax.ppermute(array, "grp", pairs)

    lane = local_call(
        lane_kernel,
        "lane",
        jax.ShapeDtypeStruct((rows, width // tile_size.shape[0]), jnp.int32),
        [],
        [],
        pl.CostEstimate(flops=10**9, bytes_accessed=0, transcendentals=0),
    )

    lane, later = lax.optimization_barrier((lane, integrals))
    own = [integrals] + [swap(integrals if step == 1 else later, "blk", blk_size, step) for step in range(1, blk_size)]

    order = sorted(range(chips), key=lambda step: (step != 0, step != chips // 2, -step))
    block = jax.ShapeDtypeStruct((rows, CORES * depth), amplitudes.dtype)
    blocks = local_call(
        functools.partial(mask_kernel, tuple(order)),
        "live_blocks",
        [block] * chips,
        [VMEM, SMEM, SMEM, VMEM],
        [lane, tile_mask, tile_size, amplitudes],
    )
    blocks = list(blocks)
    if blk_size > 1:
        blocks[-1], own[1] = lax.optimization_barrier((blocks[-1], own[1]))
    received = [blocks[0]] + [swap(b, "grp", grp_size, CORES * step) for b, step in zip(blocks[1:], order[1:])]

    other = []
    for step in range(blk_size):
        places = range(1, chips) if step > 1 else range(1, min(2, chips))
        own[step] = after(received, places, own[step])
        other.append(swap(own[step], "grp", grp_size, 1))

    partial = local_call(
        functools.partial(dot_kernel, chips, blk_size),
        "dots",
        jax.ShapeDtypeStruct((chips * rows, blk_size * cols), jnp.float32),
        [VMEM] * (chips + 2 * blk_size),
        [*received, *own, *other],
    )
    ladder = partial[:rows]
    for step in range(1, chips):
        place = 0
        for k in range(chips):
            place = jnp.where(chip == k, order.index(k ^ after_chip[step][k]), place)
        ladder += shift(lax.dynamic_slice_in_dim(partial, place * rows, rows), step)
    return ladder.astype(jnp.bfloat16)


def solution(mesh):
    return jax.shard_map(
        functools.partial(body, mesh.shape["blk"], mesh.shape["grp"]),
        mesh=mesh,
        in_specs=(P(("blk", "grp"), None), P("grp", "blk"), P(("blk", "grp"), None), P()),
        out_specs=P(("blk", "grp"), None),
        check_vma=False,
    )
```

```python
import functools
import math

import jax
import jax.numpy as jnp
from jax import lax
from jax.experimental import pallas as pl
from jax.experimental.pallas import tpu as pltpu
from jax.sharding import PartitionSpec as P

CORES = 2
VMEM = pl.BlockSpec(memory_space=pltpu.VMEM)
SMEM = pl.BlockSpec(memory_space=pltpu.SMEM)


def local_call(kernel, name, out_shape, in_specs, operands, cost=None):
    arrays = [*operands, *jax.tree.leaves(out_shape)]
    held = sum(math.prod(a.shape) * a.dtype.itemsize for a in arrays)
    return pl.pallas_call(
        kernel,
        out_shape=out_shape,
        in_specs=in_specs,
        out_specs=jax.tree.map(lambda _: VMEM, out_shape),
        name=name,
        cost_estimate=cost,
        compiler_params=pltpu.CompilerParams(vmem_limit_bytes=held + (2 << 20)),
    )(*operands)


def lane_kernel(lane_ref):
    lane_ref[...] = lax.broadcasted_iota(jnp.int32, lane_ref.shape, 1)


def mask_kernel(order, lane_ref, mask_ref, size_ref, amplitude_ref, *out_refs):
    grp = lax.axis_index("grp")
    chip, core = grp // CORES, lax.rem(grp, CORES)
    lane = lane_ref[...]
    tile = lane.shape[1]
    tiles = out_refs[0].shape[1] // tile // CORES
    for out_ref, step in zip(out_refs, order):
        for half in range(CORES):
            first = ((chip ^ step) * CORES + (core ^ half)) * tiles
            for t in range(tiles):
                k = first + t
                live = jnp.where(mask_ref[0, k] == 1, size_ref[k], 0)
                value = amplitude_ref[:, pl.ds(pl.multiple_of(k * tile, tile), tile)]
                place = (half * tiles + t) * tile
                out_ref[:, place : place + tile] = jnp.where(lane < live, value, jnp.zeros_like(value))


def dot_kernel(members, first, blocks, early, *refs):
    live_refs, own_refs, other_refs = refs[:members], refs[members : members + blocks], refs[members + blocks :][:blocks]
    out_ref = refs[-1]
    blk = lax.axis_index("blk")
    depth, cols = own_refs[0].shape
    live = jnp.concatenate([ref[...] for ref in live_refs], axis=0)
    for k in range(first if early is False else 0):
        place = pl.ds(pl.multiple_of((blk ^ k) * cols, cols), cols)
        out_ref[:, place] = refs[-2][:, k * cols : (k + 1) * cols]
    for step, (own_ref, other_ref) in enumerate(zip(own_refs, other_refs), first):
        total = jnp.dot(live[:, :depth], own_ref[...], preferred_element_type=jnp.float32)
        total += jnp.dot(live[:, depth:], other_ref[...], preferred_element_type=jnp.float32)
        if early:
            out_ref[:, step * cols : (step + 1) * cols] = total
        else:
            out_ref[:, pl.ds(pl.multiple_of((blk ^ step) * cols, cols), cols)] = total


def after(received, places, value):
    *arrived, value = lax.optimization_barrier((*[received[k] for k in places], value))
    for k, array in zip(places, arrived):
        received[k] = array
    return value


def body(blk_size, grp_size, amplitudes, integrals, tile_mask, tile_size):
    rows, width = amplitudes.shape
    depth, cols = integrals.shape
    chips = grp_size // CORES
    chip = lax.axis_index("grp") // CORES

    def swap(array, axis, size, step):
        return lax.ppermute(array, axis, [(k, k ^ step) for k in range(size)])

    ring = [k ^ (k >> 1) for k in range(chips)]
    after_chip = [[ring[(ring.index(k) + step) % chips] for k in range(chips)] for step in range(chips)]

    def shift(array, step):
        pairs = [(k, after_chip[step][k // CORES] * CORES + k % CORES) for k in range(grp_size)]
        return lax.ppermute(array, "grp", pairs)

    lane = local_call(
        lane_kernel,
        "lane",
        jax.ShapeDtypeStruct((rows, width // tile_size.shape[0]), jnp.int32),
        [],
        [],
        pl.CostEstimate(flops=10**9, bytes_accessed=0, transcendentals=0),
    )

    lane, later = lax.optimization_barrier((lane, integrals))
    own = [integrals] + [swap(integrals if step == 1 else later, "blk", blk_size, step) for step in range(1, blk_size)]

    order = sorted(range(chips), key=lambda step: (step != 0, step != chips // 2, -step))
    block = jax.ShapeDtypeStruct((rows, CORES * depth), amplitudes.dtype)
    blocks = local_call(
        functools.partial(mask_kernel, tuple(order)),
        "live_blocks",
        [block] * chips,
        [VMEM, SMEM, SMEM, VMEM],
        [lane, tile_mask, tile_size, amplitudes],
    )
    blocks = list(blocks)
    if blk_size > 1:
        blocks[-1], own[1] = lax.optimization_barrier((blocks[-1], own[1]))
    received = [blocks[0]] + [swap(b, "grp", grp_size, CORES * step) for b, step in zip(blocks[1:], order[1:])]

    other = []
    for step in range(blk_size):
        places = range(1, chips) if step > 1 else range(1, min(2, chips))
        own[step] = after(received, places, own[step])
        other.append(swap(own[step], "grp", grp_size, 1))

    first = blk_size // 2
    shape = lambda count: jax.ShapeDtypeStruct((chips * rows, count * cols), jnp.float32)
    head = local_call(
        functools.partial(dot_kernel, chips, 0, first, True),
        "dots_first",
        shape(first),
        [VMEM] * (chips + 2 * first),
        [*received, *own[:first], *other[:first]],
    )
    rest = blk_size - first
    partial = local_call(
        functools.partial(dot_kernel, chips, first, rest, False),
        "dots_rest",
        shape(blk_size),
        [VMEM] * (chips + 2 * rest + 1),
        [*received, *own[first:], *other[first:], head],
    )
    ladder = partial[:rows]
    for step in range(1, chips):
        place = 0
        for k in range(chips):
            place = jnp.where(chip == k, order.index(k ^ after_chip[step][k]), place)
        ladder += shift(lax.dynamic_slice_in_dim(partial, place * rows, rows), step)
    return ladder.astype(jnp.bfloat16)


def solution(mesh):
    return jax.shard_map(
        functools.partial(body, mesh.shape["blk"], mesh.shape["grp"]),
        mesh=mesh,
        in_specs=(P(("blk", "grp"), None), P("grp", "blk"), P(("blk", "grp"), None), P()),
        out_specs=P(("blk", "grp"), None),
        check_vma=False,
    )
```

```python
import functools
import math

import jax
import jax.numpy as jnp
from jax import lax
from jax.experimental import pallas as pl
from jax.experimental.pallas import tpu as pltpu
from jax.sharding import PartitionSpec as P

CORES = 2
VMEM = pl.BlockSpec(memory_space=pltpu.VMEM)
SMEM = pl.BlockSpec(memory_space=pltpu.SMEM)


def local_call(kernel, name, out_shape, in_specs, operands, cost=None):
    arrays = [*operands, *jax.tree.leaves(out_shape)]
    held = sum(math.prod(a.shape) * a.dtype.itemsize for a in arrays)
    return pl.pallas_call(
        kernel,
        out_shape=out_shape,
        in_specs=in_specs,
        out_specs=jax.tree.map(lambda _: VMEM, out_shape),
        name=name,
        cost_estimate=cost,
        compiler_params=pltpu.CompilerParams(vmem_limit_bytes=held + (2 << 20)),
    )(*operands)


def lane_kernel(lane_ref):
    lane_ref[...] = lax.broadcasted_iota(jnp.int32, lane_ref.shape, 1)


def mask_kernel(order, lane_ref, mask_ref, size_ref, amplitude_ref, *out_refs):
    grp = lax.axis_index("grp")
    chip, core = grp // CORES, lax.rem(grp, CORES)
    lane = lane_ref[...]
    tile = lane.shape[1]
    tiles = out_refs[0].shape[1] // tile // CORES
    for out_ref, step in zip(out_refs, order):
        for half in range(CORES):
            first = ((chip ^ step) * CORES + (core ^ half)) * tiles
            for t in range(tiles):
                k = first + t
                live = jnp.where(mask_ref[0, k] == 1, size_ref[k], 0)
                value = amplitude_ref[:, pl.ds(pl.multiple_of(k * tile, tile), tile)]
                place = (half * tiles + t) * tile
                out_ref[:, place : place + tile] = jnp.where(lane < live, value, jnp.zeros_like(value))


def dot_kernel(members, first, blocks, early, *refs):
    live_refs, own_refs, other_refs = refs[:members], refs[members : members + blocks], refs[members + blocks :][:blocks]
    out_ref = refs[-1]
    blk = lax.axis_index("blk")
    depth, cols = own_refs[0].shape
    live = jnp.concatenate([ref[...] for ref in live_refs], axis=0)
    done = 0
    for ref in () if early else refs[members + 2 * blocks : -1]:
        for k in range(ref.shape[1] // cols):
            place = pl.ds(pl.multiple_of((blk ^ done) * cols, cols), cols)
            out_ref[:, place] = ref[:, k * cols : (k + 1) * cols]
            done += 1
    for step, (own_ref, other_ref) in enumerate(zip(own_refs, other_refs), first):
        total = jnp.dot(live[:, :depth], own_ref[...], preferred_element_type=jnp.float32)
        total += jnp.dot(live[:, depth:], other_ref[...], preferred_element_type=jnp.float32)
        if early:
            out_ref[:, (step - first) * cols : (step - first + 1) * cols] = total
        else:
            out_ref[:, pl.ds(pl.multiple_of((blk ^ step) * cols, cols), cols)] = total


def after(received, places, value):
    *arrived, value = lax.optimization_barrier((*[received[k] for k in places], value))
    for k, array in zip(places, arrived):
        received[k] = array
    return value


def body(blk_size, grp_size, amplitudes, integrals, tile_mask, tile_size):
    rows, width = amplitudes.shape
    depth, cols = integrals.shape
    chips = grp_size // CORES
    chip = lax.axis_index("grp") // CORES

    def swap(array, axis, size, step):
        return lax.ppermute(array, axis, [(k, k ^ step) for k in range(size)])

    ring = [k ^ (k >> 1) for k in range(chips)]
    after_chip = [[ring[(ring.index(k) + step) % chips] for k in range(chips)] for step in range(chips)]

    def shift(array, step):
        pairs = [(k, after_chip[step][k // CORES] * CORES + k % CORES) for k in range(grp_size)]
        return lax.ppermute(array, "grp", pairs)

    lane = local_call(
        lane_kernel,
        "lane",
        jax.ShapeDtypeStruct((rows, width // tile_size.shape[0]), jnp.int32),
        [],
        [],
        pl.CostEstimate(flops=10**9, bytes_accessed=0, transcendentals=0),
    )

    lane, later = lax.optimization_barrier((lane, integrals))
    own = [integrals] + [swap(integrals if step == 1 else later, "blk", blk_size, step) for step in range(1, blk_size)]

    order = sorted(range(chips), key=lambda step: (step != 0, step != chips // 2, -step))
    block = jax.ShapeDtypeStruct((rows, CORES * depth), amplitudes.dtype)
    blocks = local_call(
        functools.partial(mask_kernel, tuple(order)),
        "live_blocks",
        [block] * chips,
        [VMEM, SMEM, SMEM, VMEM],
        [lane, tile_mask, tile_size, amplitudes],
    )
    blocks = list(blocks)
    if blk_size > 1:
        blocks[-1], own[1] = lax.optimization_barrier((blocks[-1], own[1]))
    received = [blocks[0]] + [swap(b, "grp", grp_size, CORES * step) for b, step in zip(blocks[1:], order[1:])]

    other = []
    for step in range(blk_size):
        places = range(1, chips) if step > 1 else range(1, min(2, chips))
        own[step] = after(received, places, own[step])
        other.append(swap(own[step], "grp", grp_size, 1))

    shape = lambda count: jax.ShapeDtypeStruct((chips * rows, count * cols), jnp.float32)
    cuts = [0, blk_size // 2, blk_size - 1, blk_size]
    heads = []
    for low, high in zip(cuts[:-1], cuts[1:]):
        last = high == blk_size
        heads.append(
            local_call(
                functools.partial(dot_kernel, chips, low, high - low, not last),
                f"dots_{low}",
                shape(blk_size if last else high - low),
                [VMEM] * (chips + 2 * (high - low) + len(heads) * last),
                [*received, *own[low:high], *other[low:high], *(heads if last else [])],
            )
        )
    partial = heads[-1]
    ladder = partial[:rows]
    for step in range(1, chips):
        place = 0
        for k in range(chips):
            place = jnp.where(chip == k, order.index(k ^ after_chip[step][k]), place)
        ladder += shift(lax.dynamic_slice_in_dim(partial, place * rows, rows), step)
    return ladder.astype(jnp.bfloat16)


def solution(mesh):
    return jax.shard_map(
        functools.partial(body, mesh.shape["blk"], mesh.shape["grp"]),
        mesh=mesh,
        in_specs=(P(("blk", "grp"), None), P("grp", "blk"), P(("blk", "grp"), None), P()),
        out_specs=P(("blk", "grp"), None),
        check_vma=False,
    )
```
